256 devices in a mesh: dp: 2 (over y_hi), expert: 128 (over z, x, y_lo, core).
Axes of the slice: x: 4, y: 4 (y_hi: 2, y_lo: 2; y = y_hi * 2 + y_lo), z: 8, core: 2. Of those that a mesh axis runs over, the one named last changes fastest.
Arguments:
- tokens: bfloat16 [4096, 2880], P(('dp', 'expert')), may hold values from -6 to 6
- grad_out: bfloat16 [4096, 2880], P(('dp', 'expert')), may hold values from -6 to 6
- route_ids: int32 [4096, 4], P(('dp', 'expert')), may hold values from 0 to 39, all different within a row; in each aligned block of 16 rows (0 to 15, 16 to 31, ...) at most 2 rows name the same one
- route_prob: float32 [4096, 4], P(('dp', 'expert')), may hold values from 0.05 to 1
- device_expert: int32 [128], replicated, may hold values from 0 to 39, as said below
- unit_count: int32 [128], replicated, may hold values from 264 to 480, as said below
- expert_weights: bfloat16 [128, 480, 8640], P('expert'), may hold values from -0.109375 to 0.109375
Outputs:
- grad_tokens: bfloat16 [4096, 2880], P(('dp', 'expert'))
- grad_weights: bfloat16 [128, 480, 8640], P('expert', 'dp')
The draws below stay inside these ranges and needn't reach their ends.
Inputs may be any that keep to these rules, and one draw needn't show every extreme that they name: `route_ids`: each row names 4 different experts; the 16 rows of one device name each expert at most 2 times, and in every draw some device names some expert exactly 2 times. `device_expert`: aligned blocks of 16 indices of expert hold 5 experts, ids rising by one from 5 times the block's number; the indices of one expert are consecutive, 3 or 4 of them; every expert has a group. `unit_count`: the counts of the indices of one expert sum to 1440; rows of expert_weights at or past a slot's count are not part of the model.
All inputs are finite; a program needn't handle non-finite values.
Results may differ from the reference program's by a relative error of at most 0.0058.
Values may be sent and summed in bfloat16 or wider, within the bound.
No kernel may reach another device: no remote copies, remote signals or barrier semaphores. Data moves between devices by JAX's collectives and lax.ppermute only.
A program may use at most 128 MiB of HBM per device.

```python
import math
import jax
import jax.numpy as jnp
import numpy as np
from jax import lax

D = 2880
HID = 1440
TOPK = 4
TOK_DEV = 16
SLOT = 480
EXPERTS = 40
CAP = 2
TOKENS = 4096
N_DP = 2
N_EXPERT = 128


def plan_tables(key):
    blocks = N_EXPERT // 16
    larger = jax.random.randint(jax.random.fold_in(key, 11), (blocks,), 0, 5)
    group_sizes = 3 + (jnp.arange(5)[None, :] == larger[:, None]).astype(jnp.int32)
    group_ends = jnp.cumsum(group_sizes, axis=1)
    position = jnp.arange(16)
    local_id = jnp.sum((position[None, :, None] >= group_ends[:, None, :]).astype(jnp.int32), axis=2)
    experts = local_id + 5 * jnp.arange(blocks)[:, None]
    group_begin = jnp.take_along_axis(group_ends - group_sizes, local_id, axis=1)
    member = position[None, :] - group_begin
    group_size = jnp.take_along_axis(group_sizes, local_id, axis=1)
    unit_step = HID // 60
    shifts = jax.random.randint(jax.random.fold_in(key, 12), (blocks, 2), -4, 5) * unit_step
    shifts = shifts.at[0, 0].set(4 * unit_step)
    base_units = HID // 4
    parity_sign = 1 - 2 * (member % 2)
    pair_id = jnp.minimum(member // 2, 1)
    four_counts = base_units + parity_sign * jnp.take_along_axis(shifts, pair_id, axis=1)
    counts = jnp.where(group_size == 4, four_counts, HID // 3)
    return (experts.reshape(-1).astype(jnp.int32), counts.reshape(-1).astype(jnp.int32))


def draw_device_expert(key, part):
    return plan_tables(key)[0]


def draw_unit_count(key, part):
    return plan_tables(key)[1]


def block_levels(own_key, shape, pieces, low, largest):
    def one(axis_at, shards_of):
        draws = jax.random.uniform(jax.random.fold_in(jax.random.fold_in(own_key, 6), axis_at), (shards_of,), jnp.float32, low / len(pieces), largest / len(pieces))
        return jnp.repeat(jnp.exp(draws), shape[axis_at] // shards_of).reshape((-1,) + (1,) * (len(shape) - axis_at - 1))

    loudness = one(*pieces[0])
    for cut in pieces[1:]:
        loudness = loudness * one(*cut)
    return loudness


def routed_block(rng, own, number, rows, amount, top, limit, lean):
    order = jax.random.permutation(rng, amount)
    heavy_load, common = portions_of(amount, rows * top, limit, lean, True), portions_of(amount, rows * top, limit, lean, False)
    places = jnp.arange(amount)

    def named(tallies, rotation):
        used = int((tallies > 0).sum())
        fixed = max(1, used // 4)
        shifted = fixed + (places - fixed + rotation * (used - fixed)) % max(1, amount - fixed)
        return jnp.zeros((amount,), jnp.int32).at[order[jnp.where(places < fixed, places, shifted)]].set(jnp.asarray(tallies, jnp.int32))

    tallies = jnp.where(number % 4 == 0, named(heavy_load, number // 4), named(common, number - number // 4 - 1))
    mixed = jax.random.permutation(jax.random.fold_in(own, 3), amount)
    donor, taker = mixed[0:amount // 2 * 2:2], mixed[1:amount // 2 * 2:2]
    margin = jnp.minimum(tallies[donor] - 1, limit - tallies[taker]) // 2
    margin = jnp.where((donor == order[0]) | (taker == order[0]) | (tallies[taker] == 0), 0, jnp.maximum(margin, 0))
    shifted = jax.random.randint(jax.random.fold_in(own, 4), (amount // 2,), 0, 1 << 20) % (margin + 1)
    tallies = tallies.at[donor].add(-shifted).at[taker].add(shifted)
    labels = jnp.searchsorted(jnp.cumsum(tallies), jnp.arange(rows * top), side="right").astype(jnp.int32)
    grid = labels.reshape(top, rows).T
    grid = grid[jax.random.permutation(jax.random.fold_in(own, 1), rows)]
    rotation = jax.random.randint(jax.random.fold_in(own, 2), (rows, 1), 0, top)
    return jnp.take_along_axis(grid, (jnp.arange(top)[None, :] + rotation) % top, axis=1)


def portions_of(amount, total, most, skew, full):
    weights = [(1 << 20) // math.isqrt(rank ** skew) + 1 for rank in range(1, amount + 1)]
    largest = most if full else min(most, max(-(-total // amount), total * weights[0] // sum(weights)))
    least = 1 if total - largest >= amount - 1 else 0
    given, rest = [largest] + [least] * (amount - 1), total - largest - least * (amount - 1)
    while rest > 0:
        movable = [i for i in range(1, amount) if given[i] < largest] or [i for i in range(1, amount) if given[i] < most]
        whole, budget = sum([weights[i] for i in movable]), rest
        for i in movable:
            addition = min(most - given[i], max(1, budget * weights[i] // whole), rest)
            given[i] = given[i] + addition
            rest = rest - addition
    return np.array(given)


def bell_draw(rng, extent, deviation, bound, pieces=(), kind=jnp.bfloat16):
    values = deviation * jax.random.normal(rng, extent, jnp.float32)
    if pieces:
        values = values * block_levels(rng, extent, pieces, -0.22, 0.18)
    return jnp.clip(values, -bound, bound).astype(kind)


def setup_inputs(seed: int = 0) -> dict:
    keys = jax.random.split(jax.random.key(seed), 8)
    tokens = bell_draw(keys[0], (TOKENS, D), 1.0, 6.0, ((0, 256),))
    grad_out = bell_draw(keys[1], (TOKENS, D), 1.0, 6.0, ((0, 256),))
    route_ids_keys = jax.random.split(jax.random.fold_in(keys[2], 1), TOKENS // TOK_DEV)
    route_ids_turns = jax.random.permutation(jax.random.fold_in(keys[2], 3), TOKENS // TOK_DEV)
    route_ids = jax.vmap(lambda own, number: routed_block(jax.random.fold_in(keys[2], 2), own, number, TOK_DEV, EXPERTS, TOPK, CAP, 1))(route_ids_keys, route_ids_turns).reshape((TOKENS, TOPK))
    route_prob = jnp.clip(jnp.exp(math.log(1.0) - 2.9957323 * jax.random.uniform(keys[3], (TOKENS, TOPK), jnp.float32) ** block_levels(keys[3], (TOKENS, TOPK), ((0, 256),), -0.2, 0.2)), 0.05, 1.0)
    device_expert = draw_device_expert(jax.random.fold_in(keys[7], 71), 0)
    unit_count = draw_unit_count(jax.random.fold_in(keys[7], 71), 0)
    expert_weights = bell_draw(keys[6], (N_EXPERT, SLOT, 3 * D), D ** -0.5, 0.109375, ((0, 128),))
    return dict(tokens=tokens, grad_out=grad_out, route_ids=route_ids, route_prob=route_prob, device_expert=device_expert, unit_count=unit_count, expert_weights=expert_weights)


def silu_parts(preact):
    sigma = jax.nn.sigmoid(preact)
    return preact * sigma, sigma * (1.0 + preact * (1.0 - sigma))


def route_table(ids_block, prob_block):
    flat_ids = ids_block.reshape(-1)
    onehot = (flat_ids[:, None] == jnp.arange(EXPERTS, dtype=jnp.int32)[None, :]).astype(jnp.int32)
    rank_of = jnp.sum(onehot * jnp.cumsum(onehot, axis=0), axis=1) - 1
    matched = (flat_ids[None, None, :] == jnp.arange(EXPERTS, dtype=jnp.int32)[:, None, None]) & (rank_of[None, None, :] == jnp.arange(CAP, dtype=jnp.int32)[None, :, None])
    owner = jnp.arange(flat_ids.shape[0], dtype=jnp.int32) // TOPK
    token_ids = jnp.sum(jnp.where(matched, owner[None, None, :], 0), axis=2).astype(jnp.int32)
    route_weight = jnp.sum(jnp.where(matched, prob_block.reshape(-1)[None, None, :], 0.0), axis=2)
    live_slot = jnp.any(matched, axis=2)
    return token_ids, route_weight, live_slot


def reference(tokens, grad_out, route_ids, route_prob, device_expert, unit_count, expert_weights):
    sources = N_DP * N_EXPERT
    token_ids, route_weight, live_slot = jax.vmap(route_table)(route_ids.reshape(sources, TOK_DEV, TOPK), route_prob.reshape(sources, TOK_DEV, TOPK))
    token_ids = token_ids + (jnp.arange(sources, dtype=jnp.int32) * TOK_DEV)[:, None, None]
    contract = (((1,), (1,)), ((), ()))
    rows_first = (((0,), (0,)), ((), ()))

    def one_slot(accum, slot_index):
        expert_id = device_expert[slot_index]
        slot_weights = expert_weights[slot_index]
        row_index = jnp.take(token_ids, expert_id, axis=1).reshape(-1).astype(jnp.int32)
        row_scale = jnp.take(route_weight, expert_id, axis=1).reshape(-1)
        row_live = jnp.take(live_slot, expert_id, axis=1).reshape(-1)
        token_rows = jnp.where(row_live[:, None], tokens[row_index], jnp.zeros((), tokens.dtype))
        grad_rows = jnp.where(row_live[:, None], row_scale[:, None] * grad_out[row_index].astype(jnp.float32), 0.0).astype(jnp.bfloat16)
        gate_rows = slot_weights[:, :D]
        up_rows = slot_weights[:, D:2 * D]
        down_rows = slot_weights[:, 2 * D:]
        gate_pre = lax.dot_general(token_rows, gate_rows, contract, preferred_element_type=jnp.float32)
        up_pre = lax.dot_general(token_rows, up_rows, contract, preferred_element_type=jnp.float32)
        back_grad = lax.dot_general(grad_rows, down_rows, contract, preferred_element_type=jnp.float32)
        unit_mask = (jnp.arange(SLOT, dtype=jnp.int32) < unit_count[slot_index]).astype(jnp.float32)
        active, slope = silu_parts(gate_pre)
        hidden = (active * up_pre * unit_mask).astype(jnp.bfloat16)
        grad_gate = (back_grad * up_pre * slope * unit_mask).astype(jnp.bfloat16)
        grad_up = (back_grad * active * unit_mask).astype(jnp.bfloat16)
        partial_value = jnp.dot(grad_gate, gate_rows, preferred_element_type=jnp.float32) + jnp.dot(grad_up, up_rows, preferred_element_type=jnp.float32)
        accum = accum.at[row_index].add(jnp.where(row_live[:, None], partial_value, 0.0))
        grad_slot = jnp.concatenate([
            lax.dot_general(grad_gate, token_rows, rows_first, preferred_element_type=jnp.float32),
            lax.dot_general(grad_up, token_rows, rows_first, preferred_element_type=jnp.float32),
            lax.dot_general(hidden, grad_rows, rows_first, preferred_element_type=jnp.float32)], axis=1)
        return accum, grad_slot.astype(jnp.bfloat16)

    accum, grad_slots = lax.scan(one_slot, jnp.zeros((TOKENS, D), jnp.float32), jnp.arange(N_EXPERT, dtype=jnp.int32))
    return accum.astype(jnp.bfloat16), grad_slots
```

```python
import jax
import jax.numpy as jnp
from jax import lax
from jax.sharding import PartitionSpec as P

F32 = jnp.float32
BF16 = jnp.bfloat16


def dot(left, right, left_dim, right_dim):
    return lax.dot_general(
        left, right, (((left_dim,), (right_dim,)), ((), ())), preferred_element_type=F32
    )


def swap_dp(value):
    return lax.ppermute(value, "dp", [(0, 1), (1, 0)])


def shards(tokens, grad_out, route_ids, route_prob, device_expert, unit_count, expert_weights):
    token_count, width = tokens.shape
    top_count = route_ids.shape[1]
    devices = lax.axis_size("expert")
    capacity = token_count * top_count * 4 // devices
    flat_ids = route_ids.reshape(-1)
    routes = jnp.arange(flat_ids.shape[0], dtype=jnp.int32)
    earlier = (flat_ids[:, None] == flat_ids[None, :]) & (routes[None, :] < routes[:, None])
    rank_of = jnp.sum(earlier.astype(jnp.int32), axis=1)
    picked = (flat_ids[None, None, :] == device_expert[:, None, None]) & (
        rank_of[None, None, :] == jnp.arange(capacity, dtype=jnp.int32)[None, :, None]
    )
    picked = picked.astype(F32).reshape(devices * capacity, token_count * top_count)
    by_token = picked.reshape(devices * capacity, token_count, top_count).sum(axis=2).astype(BF16)
    route_scale = jnp.sum(picked * route_prob.reshape(-1)[None, :], axis=1)
    sent_rows = dot(by_token, tokens, 1, 0).astype(BF16)
    sent_grads = (route_scale[:, None] * dot(by_token, grad_out, 1, 0)).astype(BF16)
    outgoing = jnp.stack(
        [
            sent_rows.reshape(devices, capacity, width),
            sent_grads.reshape(devices, capacity, width),
        ],
        axis=1,
    )
    arrived = lax.all_to_all(outgoing, "expert", split_axis=0, concat_axis=0, tiled=True)
    token_rows = arrived[:, 0].reshape(-1, width)
    grad_rows = arrived[:, 1].reshape(-1, width)
    other_token_rows = swap_dp(token_rows)
    other_grad_rows = swap_dp(grad_rows)

    position = lax.axis_index("expert")
    replica = lax.axis_index("dp")
    unit_limit = lax.dynamic_index_in_dim(unit_count, position, keepdims=False)
    slot_weights = expert_weights[0]
    slot_units = slot_weights.shape[0]
    unit_mask = (jnp.arange(slot_units, dtype=jnp.int32) < unit_limit).astype(F32)[:, None]
    gate_w = slot_weights[:, :width]
    up_w = slot_weights[:, width : 2 * width]
    down_w = slot_weights[:, 2 * width :]
    gate_pre = dot(gate_w, token_rows, 1, 1)
    up_pre = dot(up_w, token_rows, 1, 1)
    back_grad = dot(down_w, grad_rows, 1, 1)
    sigma = jax.nn.sigmoid(gate_pre)
    active = gate_pre * sigma
    slope = sigma * (1.0 + gate_pre * (1.0 - sigma))
    hidden = (active * up_pre * unit_mask).astype(BF16)
    grad_gate = (back_grad * up_pre * slope * unit_mask).astype(BF16)
    grad_up = (back_grad * active * unit_mask).astype(BF16)
    units = jnp.stack([grad_gate, grad_up, hidden])

    half = slot_units // 2
    own = lax.dynamic_slice_in_dim(units, replica * half, half, axis=1)
    other = swap_dp(lax.dynamic_slice_in_dim(units, (1 - replica) * half, half, axis=1))

    partial_value = (dot(grad_gate, gate_w, 0, 0) + dot(grad_up, up_w, 0, 0)).astype(BF16)
    returned = lax.all_to_all(
        partial_value.reshape(devices, capacity, width),
        "expert",
        split_axis=0,
        concat_axis=0,
        tiled=True,
    )
    grad_tokens = dot(by_token, returned.reshape(devices * capacity, width), 0, 0).astype(BF16)

    gate_up = dot(own[:2].reshape(2 * half, -1), token_rows, 1, 0) + dot(
        other[:2].reshape(2 * half, -1), other_token_rows, 1, 0
    )
    down = dot(own[2], grad_rows, 1, 0) + dot(other[2], other_grad_rows, 1, 0)
    grad_weights = jnp.concatenate(
        [gate_up[:half].astype(BF16), gate_up[half:].astype(BF16), down.astype(BF16)], axis=1
    )
    return grad_tokens, grad_weights[None]


def solution(mesh):
    in_specs = (
        P(("dp", "expert"), None),
        P(("dp", "expert"), None),
        P(("dp", "expert"), None),
        P(("dp", "expert"), None),
        P(),
        P(),
        P("expert", None, None),
    )
    out_specs = (P(("dp", "expert"), None), P("expert", "dp", None))
    return jax.shard_map(shards, mesh=mesh, in_specs=in_specs, out_specs=out_specs, check_vma=False)
```

```python
import jax
import jax.numpy as jnp
from jax import lax
from jax.experimental import pallas as pl
from jax.experimental.pallas import tpu as pltpu
from jax.sharding import Mesh, PartitionSpec as P

F32 = jnp.float32
BF16 = jnp.bfloat16
D = 2880
WIDE = 2944
EDGE = 2816
LAST = D - EDGE
TOKENS = 16
TOPK = 4
PLANES = 8
PEERS = 16
GROUP = 5
SLOTS = 2 * GROUP
PACKED = 24
ROWS = 256
GATHERED = PLANES * 16
UNITS = 480
HALF = 240
STEP = 512
PLANE = ("x", "y", "c")
ALL = ("dp", "z", "x", "y", "c")

VMEM = pl.BlockSpec(memory_space=pltpu.VMEM)
SMEM = pl.BlockSpec(memory_space=pltpu.SMEM)
WAITED = pl.BlockSpec(memory_space=pl.ANY)


def dot(left, right, left_dim, right_dim):
    return lax.dot_general(
        left, right, (((left_dim,), (right_dim,)), ((), ())), preferred_element_type=F32
    )


def chunks(total):
    return [(at, min(STEP, total - at)) for at in range(0, total, STEP)]


def iota(shape, dim):
    return lax.broadcasted_iota(jnp.int32, shape, dim)


def call(kernel, out_shape, in_specs, flops, moved, scratch=(), mib=24):
    outs = jax.tree.map(lambda _: VMEM, out_shape)
    return pl.pallas_call(
        kernel,
        out_shape=out_shape,
        in_specs=in_specs,
        out_specs=outs,
        scratch_shapes=list(scratch),
        compiler_params=pltpu.CompilerParams(vmem_limit_bytes=mib << 20),
        cost_estimate=pl.CostEstimate(flops=flops, bytes_accessed=moved, transcendentals=0),
    )


def shape(dims, kind=BF16):
    return jax.ShapeDtypeStruct(dims, kind)


def pack_kernel(plane_ref, token_ref, grad_ref, id_ref, prob_ref, *out_refs):
    grid = (TOKENS, ROWS)
    row = iota(grid, 1)
    hop = (row * 2731) >> 16
    slot = row - PACKED * hop
    is_grad = slot >= SLOTS
    slot = jnp.where(is_grad, slot - SLOTS, slot)
    expert = GROUP * ((plane_ref[0] + hop) & (PLANES - 1)) + (slot >> 1)
    picked, weight = pick_tokens(id_ref, prob_ref, expert, slot)
    scale = jnp.sum(picked * weight, axis=0, keepdims=True)
    scale = jnp.where(is_grad[:1], scale, 0.0)
    scale = jnp.broadcast_to(scale, (TOKENS, ROWS)).T[:, :1]
    want_grad = jnp.where(is_grad, 1.0, 0.0).T[:, :1] > 0.5
    picked = picked.T.astype(BF16)
    for at, size in chunks(WIDE):
        end = min(at + size, D)
        value = jnp.where(
            want_grad,
            scale * dot(picked, grad_ref[:, at:end], 1, 0),
            dot(picked, token_ref[:, at:end], 1, 0),
        )
        if end < at + size:
            value = jnp.concatenate([value, jnp.zeros((ROWS, at + size - end), F32)], axis=1)
        for k, out_ref in enumerate(out_refs):
            out_ref[:, at : at + size] = value[PACKED * k : PACKED * (k + 1)].astype(BF16)


def pick_tokens(id_ref, prob_ref, expert, slot):
    has = jnp.zeros(expert.shape, F32)
    weight = jnp.zeros(expert.shape, F32)
    ids = id_ref[...]
    for k in range(TOPK):
        match = ids[:, k : k + 1] == expert
        has = jnp.where(match, 1.0, has)
        if prob_ref is not None:
            weight = jnp.where(match, prob_ref[:, k : k + 1], weight)
    square = (TOKENS, TOKENS)
    earlier = (iota(square, 1) < iota(square, 0)).astype(F32).astype(BF16)
    rank = dot(earlier, has.astype(BF16), 1, 0).astype(jnp.int32)
    wanted = (has > 0.5) & (rank == (slot & 1)) & (slot < SLOTS)
    return jnp.where(wanted, 1.0, 0.0), weight


def local_slot(expert_ref, plane_ref, row):
    local = jnp.zeros(row.shape, jnp.int32)
    for peer in range(PEERS):
        named = expert_ref[plane_ref[0] * PEERS + peer] - GROUP * plane_ref[0]
        local = jnp.where((row >> 4) == peer, named, local)
    return 2 * local + (row & 1)


def pick_kernel(expert_ref, plane_ref, *refs):
    blocks, (row_ref, grad_ref) = refs[:PLANES], refs[PLANES:]
    grid = (ROWS, ROWS)
    row, column = iota(grid, 0), iota(grid, 1)
    source = PACKED * ((row >> 1) & (PLANES - 1)) + local_slot(expert_ref, plane_ref, row)
    column = column[:, : PLANES * PACKED]
    source = source[:, : PLANES * PACKED]
    pick_row = (column == source).astype(F32).astype(BF16)
    pick_grad = (column == source + SLOTS).astype(F32).astype(BF16)
    for at, size in chunks(WIDE):
        block = jnp.concatenate(
            [ref[:, at : at + size].astype(F32) for ref in blocks], axis=0
        ).astype(BF16)
        row_ref[:, at : at + size] = dot(pick_row, block, 1, 0).astype(BF16)
        keep = min(at + size, D) - at
        grad_ref[:, at : at + keep] = dot(pick_grad, block, 1, 0)[:, :keep].astype(BF16)


def shifted(rows):
    return pltpu.roll(rows.astype(F32), LAST, 1).astype(BF16)


def unit_kernel(
    limit_ref, replica_ref, row_ref, grad_ref, weight_ref, own_ref, other_ref, part_ref, shift_ref
):
    shift_ref[...] = shifted(row_ref[...])
    gate = dot(weight_ref[:, :WIDE], row_ref[...], 1, 1)
    up = dot(weight_ref[:, EDGE : 2 * D], shift_ref[...], 1, 1)
    back = dot(weight_ref[:, 2 * D :], grad_ref[...], 1, 1)
    mask = jnp.where(iota(gate.shape, 0) < limit_ref[0], 1.0, 0.0)
    sigma = jax.nn.sigmoid(gate)
    active = gate * sigma * mask
    hidden = (active * up).astype(BF16)
    grad_gate = (back * up * (sigma * (1.0 + gate * (1.0 - sigma))) * mask).astype(BF16)
    grad_up = (back * active).astype(BF16)
    for half in range(2):
        for target, mine in ((own_ref, half), (other_ref, 1 - half)):

            @pl.when(replica_ref[0] == mine)
            def _(target=target, at=half * HALF):
                target[0] = grad_gate[at : at + HALF]
                target[1] = grad_up[at : at + HALF]
                target[2] = hidden[at : at + HALF]

    gate_rows = grad_gate.astype(F32).T.astype(BF16)
    up_rows = grad_up.astype(F32).T.astype(BF16)
    for at, size in chunks(WIDE):
        end = at + size
        value = dot(gate_rows, weight_ref[:, at:end], 1, 0)
        wide = dot(up_rows, weight_ref[:, EDGE + at : min(EDGE + end + 128, 2 * D)], 1, 0)
        value = value + pltpu.roll(wide, wide.shape[1] - LAST, 1)[:, :size]
        keep = min(end, D) - at
        part_ref[:, at : at + keep] = value[:, :keep].astype(BF16)


def weight_kernel(
    own_ref, other_ref, row_ref, far_row_ref, grad_ref, far_grad_ref, out_ref, shift_ref, far_shift_ref
):
    shift_ref[...] = shifted(row_ref[...])
    far_shift_ref[...] = shifted(far_row_ref[...])

    def term(which, near, far, at, end):
        return dot(own_ref[which], near[:, at:end], 1, 0) + dot(
            other_ref[which], far[:, at:end], 1, 0
        )

    for at, size in chunks(EDGE):
        value = term(0, row_ref, far_row_ref, at, at + size)
        out_ref[0, :, at : at + size] = value.astype(BF16)
    value = term(0, row_ref, far_row_ref, EDGE, WIDE) + term(1, shift_ref, far_shift_ref, 0, 128)
    out_ref[0, :, EDGE:WIDE] = value.astype(BF16)
    for at, size in chunks(WIDE - 128):
        value = term(1, shift_ref, far_shift_ref, 128 + at, 128 + at + size)
        out_ref[0, :, WIDE + at : WIDE + at + size] = value.astype(BF16)
    for at, size in chunks(D):
        value = term(2, grad_ref, far_grad_ref, at, at + size)
        out_ref[0, :, 2 * D + at : 2 * D + at + size] = value.astype(BF16)


def gather_kernel(expert_ref, plane_ref, part_ref, _, __, out_ref):
    grid = (GATHERED, ROWS)
    row, column = iota(grid, 0), iota(grid, 1)
    same_hop = (row >> 4) == ((column >> 1) & (PLANES - 1))
    same_slot = (row & 15) == local_slot(expert_ref, plane_ref, column)
    picked = (same_hop & same_slot).astype(F32).astype(BF16)
    for at, size in chunks(D):
        value = dot(picked, part_ref[:, at : at + size], 1, 0).astype(BF16)
        for k in range(PLANES):
            source = (plane_ref[0] + PLANES - k) & (PLANES - 1)
            out_ref[source, :, at : at + size] = value[TOKENS * k : TOKENS * (k + 1)]


def sum_kernel(part_ref, id_ref, _, out_ref):
    row = iota((TOKENS, GATHERED), 1)
    slot = row & 15
    picked, _ = pick_tokens(id_ref, None, GROUP * (row >> 4) + (slot >> 1), slot)
    picked = picked.astype(BF16)
    for at, size in chunks(D):
        value = dot(picked, part_ref[:, at : at + size], 1, 0)
        out_ref[:, at : at + size] = value.astype(BF16)


def along_z(value, by):
    return lax.ppermute(value, "z", [(i, (i + by) % PLANES) for i in range(PLANES)])


def swap_dp(value):
    return lax.ppermute(value, "dp", [(0, 1), (1, 0)])


def swap_rows(rows):
    blocks = rows.reshape(PEERS, ROWS // PEERS, rows.shape[1])
    return swap_dp(blocks).reshape(rows.shape)


def in_plane(rows):
    blocks = rows.reshape(PEERS, ROWS // PEERS, rows.shape[1])
    blocks = lax.all_to_all(blocks, PLANE, split_axis=0, concat_axis=0, tiled=True)
    return blocks.reshape(rows.shape)


FAR_FIRST = (4, 3, 5, 2, 6, 1, 7)


def to_planes(blocks):
    sent = {by: along_z(blocks[by], by) for by in FAR_FIRST}
    return [blocks[0]] + [sent[by] for by in range(1, PLANES)]


def shards(tokens, grad_out, route_ids, route_prob, device_expert, unit_count, expert_weights):
    plane = lax.axis_index("z").astype(jnp.int32)
    replica = lax.axis_index("dp").astype(jnp.int32).reshape(1)
    limit = lax.dynamic_slice_in_dim(unit_count, plane * PEERS + lax.axis_index(PLANE), 1)
    slot_weights = expert_weights[0]

    plane = plane.reshape(1)
    row_flops = 2 * ROWS * D
    packed = call(
        pack_kernel,
        [shape((PACKED, WIDE))] * PLANES,
        [SMEM] + [VMEM] * 4,
        row_flops * TOKENS,
        1_400_000,
    )(plane, tokens, grad_out, route_ids, route_prob)
    blocks = to_planes(packed)
    sent_rows, sent_grads = call(
        pick_kernel,
        (shape((ROWS, WIDE)), shape((ROWS, D))),
        [SMEM, SMEM] + [VMEM] * PLANES,
        2 * row_flops * PLANES * PACKED,
        4_200_000,
    )(device_expert, plane, *blocks)
    token_rows = in_plane(sent_rows)
    far_token_rows = swap_rows(token_rows)
    grad_rows = in_plane(sent_grads)
    far_grad_rows = swap_rows(grad_rows)

    own, other, part = call(
        unit_kernel,
        (shape((3, HALF, ROWS)), shape((3, HALF, ROWS)), shape((ROWS, D))),
        [SMEM, SMEM] + [VMEM] * 3,
        5 * row_flops * UNITS,
        14_000_000,
        [pltpu.VMEM((ROWS, WIDE), BF16)],
        40,
    )(limit, replica, token_rows, grad_rows, slot_weights)
    other = swap_dp(other)

    returned = in_plane(part)
    token_parts = call(
        gather_kernel,
        shape((PLANES, TOKENS, D)),
        [SMEM, SMEM, VMEM, WAITED, WAITED],
        row_flops * GATHERED,
        2_400_000,
    )(device_expert, plane, returned, far_token_rows, other)
    home = lax.all_to_all(token_parts, "z", split_axis=0, concat_axis=0, tiled=True)
    grad_weights = call(
        weight_kernel,
        shape((1, HALF, 3 * D)),
        [VMEM] * 6,
        3 * row_flops * UNITS,
        12_000_000,
        [pltpu.VMEM((ROWS, WIDE), BF16)] * 2,
        40,
    )(own, other, token_rows, far_token_rows, grad_rows, far_grad_rows)
    grad_tokens = call(
        sum_kernel, shape((TOKENS, D)), [VMEM, VMEM, WAITED], row_flops, 900_000
    )(home.reshape(GATHERED, D), route_ids, far_grad_rows)
    return grad_tokens, grad_weights


def solution(mesh):
    fine = Mesh(mesh.devices.reshape(2, PLANES, 4, 2, 2), ALL)
    slots = ("z",) + PLANE
    in_specs = (P(ALL), P(ALL), P(ALL), P(ALL), P(), P(), P(slots))
    out_specs = (P(ALL), P(slots, "dp"))
    return jax.shard_map(shards, mesh=fine, in_specs=in_specs, out_specs=out_specs, check_vma=False)
```

```python
import jax
import jax.numpy as jnp
from jax import lax
from jax.experimental import pallas as pl
from jax.experimental.pallas import tpu as pltpu
from jax.sharding import Mesh, PartitionSpec as P

F32 = jnp.float32
BF16 = jnp.bfloat16
D = 2880
WIDE = 2944
EDGE = 2816
LAST = D - EDGE
TOKENS = 16
TOPK = 4
PLANES = 8
PEERS = 16
GROUP = 5
SLOTS = 2 * GROUP
PACKED = 24
ROWS = 256
GATHERED = PLANES * 16
UNITS = 480
HALF = 240
STEP = 512
PLANE = ("x", "y", "c")
ALL = ("dp", "z", "x", "y", "c")

VMEM = pl.BlockSpec(memory_space=pltpu.VMEM)
SMEM = pl.BlockSpec(memory_space=pltpu.SMEM)
WAITED = pl.BlockSpec(memory_space=pl.ANY)


def dot(left, right, left_dim, right_dim):
    return lax.dot_general(
        left, right, (((left_dim,), (right_dim,)), ((), ())), preferred_element_type=F32
    )


def chunks(total):
    return [(at, min(STEP, total - at)) for at in range(0, total, STEP)]


def iota(shape, dim):
    return lax.broadcasted_iota(jnp.int32, shape, dim)


def call(kernel, out_shape, in_specs, flops, moved, scratch=(), mib=24):
    outs = jax.tree.map(lambda _: VMEM, out_shape)
    return pl.pallas_call(
        kernel,
        out_shape=out_shape,
        in_specs=in_specs,
        out_specs=outs,
        scratch_shapes=list(scratch),
        compiler_params=pltpu.CompilerParams(vmem_limit_bytes=mib << 20),
        cost_estimate=pl.CostEstimate(flops=flops, bytes_accessed=moved, transcendentals=0),
    )


def shape(dims, kind=BF16):
    return jax.ShapeDtypeStruct(dims, kind)


def stage_kernel(token_ref, grad_ref, id_ref, prob_ref, out_ref):
    out_ref[:TOKENS, :EDGE] = token_ref[:, :EDGE]
    out_ref[TOKENS:, :EDGE] = grad_ref[:, :EDGE]
    lane = iota((TOKENS, 128), 1)
    blank = jnp.zeros((TOKENS, 128 - LAST), F32)
    tail = jnp.concatenate([token_ref[:, EDGE:].astype(F32), blank], axis=1)
    grad_tail = jnp.concatenate([grad_ref[:, EDGE:].astype(F32), blank], axis=1)
    prob = prob_ref[...]
    high = prob.astype(BF16).astype(F32)
    rest = prob - high
    middle = rest.astype(BF16).astype(F32)
    for at, part in enumerate((id_ref[...].astype(F32), high, middle, rest - middle)):
        for k in range(TOPK):
            tail = jnp.where(lane == LAST + TOPK * at + k, part[:, k : k + 1], tail)
    out_ref[:TOKENS, EDGE:] = tail.astype(BF16)
    out_ref[TOKENS:, EDGE:] = grad_tail.astype(BF16)


def pack_kernel(plane_ref, raw_ref, *refs):
    out_refs = refs[-PLANES:]
    routes = raw_ref[:TOKENS, EDGE:].astype(F32)

    def fact(at):
        return routes[:, LAST + at : LAST + at + TOPK]

    ids = fact(0).astype(jnp.int32)
    prob = fact(TOPK) + (fact(2 * TOPK) + fact(3 * TOPK))
    grid = (TOKENS, ROWS)
    row = iota(grid, 1)
    hop = (row * 2731) >> 16
    slot = row - PACKED * hop
    is_grad = slot >= SLOTS
    slot = jnp.where(is_grad, slot - SLOTS, slot)
    expert = GROUP * ((plane_ref[0] + hop) & (PLANES - 1)) + (slot >> 1)
    picked, weight = pick_tokens(ids, prob, expert, slot)
    scale = jnp.sum(picked * weight, axis=0, keepdims=True)
    scale = jnp.where(is_grad[:1], scale, 0.0)
    scale = jnp.broadcast_to(scale, (TOKENS, ROWS)).T[:, :1]
    want_grad = jnp.where(is_grad, 1.0, 0.0).T[:, :1] > 0.5
    picked = picked.T.astype(BF16)
    for at, size in chunks(WIDE):
        end = min(at + size, D)
        value = jnp.where(
            want_grad,
            scale * dot(picked, raw_ref[TOKENS:, at:end], 1, 0),
            dot(picked, raw_ref[:TOKENS, at:end], 1, 0),
        )
        if end < at + size:
            value = jnp.concatenate([value, jnp.zeros((ROWS, at + size - end), F32)], axis=1)
        for k, out_ref in enumerate(out_refs):
            out_ref[:, at : at + size] = value[PACKED * k : PACKED * (k + 1)].astype(BF16)


def pick_tokens(ids, prob, expert, slot):
    has = jnp.zeros(expert.shape, F32)
    weight = jnp.zeros(expert.shape, F32)
    for k in range(TOPK):
        match = ids[:, k : k + 1] == expert
        has = jnp.where(match, 1.0, has)
        weight = jnp.where(match, prob[:, k : k + 1], weight)
    square = (TOKENS, TOKENS)
    earlier = (iota(square, 1) < iota(square, 0)).astype(F32).astype(BF16)
    rank = dot(earlier, has.astype(BF16), 1, 0).astype(jnp.int32)
    wanted = (has > 0.5) & (rank == (slot & 1)) & (slot < SLOTS)
    return jnp.where(wanted, 1.0, 0.0), weight


def local_slot(expert_ref, plane_ref, row):
    local = jnp.zeros(row.shape, jnp.int32)
    for peer in range(PEERS):
        named = expert_ref[plane_ref[0] * PEERS + peer] - GROUP * plane_ref[0]
        local = jnp.where((row >> 4) == peer, named, local)
    return 2 * local + (row & 1)


def pick_kernel(expert_ref, plane_ref, *refs):
    blocks, out_ref = refs[:PLANES], refs[-1]
    grid = (ROWS, ROWS)
    row, column = iota(grid, 0), iota(grid, 1)
    source = PACKED * ((row >> 1) & (PLANES - 1)) + local_slot(expert_ref, plane_ref, row)
    column = column[:, : PLANES * PACKED]
    source = source[:, : PLANES * PACKED]
    pick_row = (column == source).astype(F32).astype(BF16)
    pick_grad = (column == source + SLOTS).astype(F32).astype(BF16)
    for at, size in chunks(WIDE):
        block = jnp.concatenate(
            [ref[:, at : at + size].astype(F32) for ref in blocks], axis=0
        ).astype(BF16)
        for first, picked in ((0, pick_row), (16, pick_grad)):
            value = dot(picked, block, 1, 0).astype(BF16)
            out_ref[:, first : first + 16, at : at + size] = value.reshape(PEERS, 16, size)


def token_part(ref, at=0, end=WIDE):
    return ref[:, :16, at:end].reshape(ROWS, end - at)


def grad_part(ref, at=0, end=D):
    return ref[:, 16:, at:end].reshape(ROWS, end - at)


def shifted(rows):
    return pltpu.roll(rows.astype(F32), LAST, 1).astype(BF16)


def unit_kernel(
    limit_ref, replica_ref, pair_ref, weight_ref, _, own_ref, other_ref, part_ref, shift_ref
):
    rows = token_part(pair_ref)
    shift_ref[...] = shifted(rows)
    gate = dot(weight_ref[:, :WIDE], rows, 1, 1)
    up = dot(weight_ref[:, EDGE : 2 * D], shift_ref[...], 1, 1)
    back = dot(weight_ref[:, 2 * D :], grad_part(pair_ref), 1, 1)
    mask = jnp.where(iota(gate.shape, 0) < limit_ref[0], 1.0, 0.0)
    sigma = jax.nn.sigmoid(gate)
    active = gate * sigma * mask
    hidden = (active * up).astype(BF16)
    grad_gate = (back * up * (sigma * (1.0 + gate * (1.0 - sigma))) * mask).astype(BF16)
    grad_up = (back * active).astype(BF16)
    for half in range(2):
        for target, mine in ((own_ref, half), (other_ref, 1 - half)):

            @pl.when(replica_ref[0] == mine)
            def _(target=target, at=half * HALF):
                target[0] = grad_gate[at : at + HALF]
                target[1] = grad_up[at : at + HALF]
                target[2] = hidden[at : at + HALF]

    gate_rows = grad_gate.astype(F32).T.astype(BF16)
    up_rows = grad_up.astype(F32).T.astype(BF16)
    for at, size in chunks(WIDE):
        end = at + size
        value = dot(gate_rows, weight_ref[:, at:end], 1, 0)
        wide = dot(up_rows, weight_ref[:, EDGE + at : min(EDGE + end + 128, 2 * D)], 1, 0)
        value = value + pltpu.roll(wide, wide.shape[1] - LAST, 1)[:, :size]
        keep = min(end, D) - at
        part_ref[:, at : at + keep] = value[:, :keep].astype(BF16)


def weight_kernel(own_ref, other_ref, pair_ref, far_ref, out_ref, shift_ref, far_shift_ref):
    shift_ref[...] = shifted(token_part(pair_ref))
    far_shift_ref[...] = shifted(token_part(far_ref))

    def term(which, near, far):
        return dot(own_ref[which], near, 1, 0) + dot(other_ref[which], far, 1, 0)

    def gate_term(at, end):
        return term(0, token_part(pair_ref, at, end), token_part(far_ref, at, end))

    def up_term(at, end):
        return term(1, shift_ref[:, at:end], far_shift_ref[:, at:end])

    for at, size in chunks(EDGE):
        value = gate_term(at, at + size)
        out_ref[0, :, at : at + size] = value.astype(BF16)
    value = gate_term(EDGE, WIDE) + up_term(0, 128)
    out_ref[0, :, EDGE:WIDE] = value.astype(BF16)
    for at, size in chunks(WIDE - 128):
        value = up_term(128 + at, 128 + at + size)
        out_ref[0, :, WIDE + at : WIDE + at + size] = value.astype(BF16)
    for at, size in chunks(D):
        value = term(
            2, grad_part(pair_ref, at, at + size), grad_part(far_ref, at, at + size)
        )
        out_ref[0, :, 2 * D + at : 2 * D + at + size] = value.astype(BF16)


def gather_kernel(expert_ref, plane_ref, part_ref, *out_refs):
    grid = (GATHERED, ROWS)
    row, column = iota(grid, 0), iota(grid, 1)
    same_hop = (row >> 4) == ((column >> 1) & (PLANES - 1))
    same_slot = (row & 15) == local_slot(expert_ref, plane_ref, column)
    picked = (same_hop & same_slot).astype(F32).astype(BF16)
    for at, size in chunks(D):
        value = dot(picked, part_ref[:, at : at + size], 1, 0).astype(BF16)
        for k, out_ref in enumerate(out_refs):
            out_ref[:, at : at + size] = value[16 * k : 16 * (k + 1)]


def sum_kernel(plane_ref, id_ref, *refs):
    blocks, out_ref = refs[:PLANES], refs[PLANES]
    row = iota((TOKENS, GATHERED), 1)
    slot = row & 15
    expert = GROUP * ((plane_ref[0] + (row >> 4)) & (PLANES - 1)) + (slot >> 1)
    picked, _ = pick_tokens(id_ref[...], jnp.zeros((TOKENS, TOPK), F32), expert, slot)
    picked = picked.astype(BF16)
    for at, size in chunks(D):
        block = jnp.concatenate([ref[:, at : at + size] for ref in blocks], axis=0)
        out_ref[:, at : at + size] = dot(picked, block, 1, 0).astype(BF16)


def along_z(value, by):
    return lax.ppermute(value, "z", [(i, (i + by) % PLANES) for i in range(PLANES)])


def swap_dp(value):
    return lax.ppermute(value, "dp", [(0, 1), (1, 0)])


def after(value, other):
    return pl.pallas_call(
        lambda *refs: None,
        out_shape=shape(value.shape),
        in_specs=[WAITED, WAITED],
        out_specs=WAITED,
        input_output_aliases={0: 0},
    )(value, other)


def in_plane(blocks):
    return lax.all_to_all(blocks, PLANE, split_axis=0, concat_axis=0, tiled=True)


FAR_FIRST = (4, 3, 5, 2, 6, 1, 7)


def to_planes(blocks):
    sent = {by: along_z(blocks[by], by) for by in FAR_FIRST}
    return [blocks[0]] + [sent[by] for by in range(1, PLANES)]


def shards(tokens, grad_out, route_ids, route_prob, device_expert, unit_count, expert_weights):
    plane = lax.axis_index("z").astype(jnp.int32)
    replica = lax.axis_index("dp").astype(jnp.int32).reshape(1)
    limit = lax.dynamic_slice_in_dim(unit_count, plane * PEERS + lax.axis_index(PLANE), 1)
    slot_weights = expert_weights[0]

    plane = plane.reshape(1)
    row_flops = 2 * ROWS * D
    raw = call(stage_kernel, shape((2 * TOKENS, WIDE)), [VMEM] * 4, 0, 400_000, (), 8)(
        tokens, grad_out, route_ids, route_prob
    )

    def pack(block):
        return call(
            pack_kernel,
            [shape((PACKED, WIDE))] * PLANES,
            [SMEM, VMEM],
            row_flops * TOKENS,
            1_400_000,
            (),
            12,
        )(plane, block)

    def pick(blocks, *earlier):
        return call(
            pick_kernel,
            shape((PEERS, 32, WIDE)),
            [SMEM, SMEM] + [VMEM] * PLANES + [WAITED] * len(earlier),
            2 * row_flops * PLANES * PACKED,
            4_200_000,
            (),
            14,
        )(device_expert, plane, *blocks, *earlier)

    blocks = pack(raw)
    far_blocks = pack(swap_dp(raw))
    pairs = in_plane(pick(to_planes(blocks), far_blocks[0]))
    far_sent = pick(to_planes(far_blocks))

    own, other, part = call(
        unit_kernel,
        (shape((3, HALF, ROWS)), shape((3, HALF, ROWS)), shape((ROWS, D))),
        [SMEM, SMEM, VMEM, VMEM, WAITED],
        5 * row_flops * UNITS,
        14_000_000,
        [pltpu.VMEM((ROWS, WIDE), BF16)],
        28,
    )(limit, replica, pairs, slot_weights, far_sent)
    other = swap_dp(other)

    returned = in_plane(part.reshape(PEERS, 16, D)).reshape(ROWS, D)
    token_parts = call(
        gather_kernel,
        [shape((16, D))] * PLANES,
        [SMEM, SMEM, VMEM],
        row_flops * GATHERED,
        2_400_000,
    )(device_expert, plane, returned)
    home = {by: along_z(token_parts[by], -by) for by in FAR_FIRST}
    home = [token_parts[0]] + [home[by] for by in range(1, PLANES)]
    far_pairs = in_plane(after(far_sent, returned))
    grad_weights = call(
        weight_kernel,
        shape((1, HALF, 3 * D)),
        [VMEM] * 4,
        3 * row_flops * UNITS,
        12_000_000,
        [pltpu.VMEM((ROWS, WIDE), BF16)] * 2,
        24,
    )(own, other, pairs, far_pairs)
    grad_tokens = call(
        sum_kernel, shape((TOKENS, D)), [SMEM] + [VMEM] * (1 + PLANES), row_flops, 900_000
    )(plane, route_ids, *home)
    return grad_tokens, grad_weights


def solution(mesh):
    fine = Mesh(mesh.devices.reshape(2, PLANES, 4, 2, 2), ALL)
    slots = ("z",) + PLANE
    in_specs = (P(ALL), P(ALL), P(ALL), P(ALL), P(), P(), P(slots))
    out_specs = (P(ALL), P(slots, "dp"))
    return jax.shard_map(shards, mesh=fine, in_specs=in_specs, out_specs=out_specs, check_vma=False)
```

```python
import jax
import jax.numpy as jnp
from jax import lax
from jax.experimental import pallas as pl
from jax.experimental.pallas import tpu as pltpu
from jax.sharding import Mesh, PartitionSpec as P

F32 = jnp.float32
BF16 = jnp.bfloat16
D = 2880
WIDE = 2944
EDGE = 2816
LAST = D - EDGE
TOKENS = 16
TOPK = 4
PLANES = 8
PEERS = 16
GROUP = 5
SLOTS = 2 * GROUP
PACKED = 24
ROWS = 256
GATHERED = PLANES * 16
UNITS = 480
HALF = 240
STEP = 512
PLANE = ("x", "y", "c")
ALL = ("dp", "z", "x", "y", "c")

VMEM = pl.BlockSpec(memory_space=pltpu.VMEM)
SMEM = pl.BlockSpec(memory_space=pltpu.SMEM)
WAITED = pl.BlockSpec(memory_space=pl.ANY)


def dot(left, right, left_dim, right_dim):
    return lax.dot_general(
        left, right, (((left_dim,), (right_dim,)), ((), ())), preferred_element_type=F32
    )


def chunks(total):
    return [(at, min(STEP, total - at)) for at in range(0, total, STEP)]


def iota(shape, dim):
    return lax.broadcasted_iota(jnp.int32, shape, dim)


def call(kernel, out_shape, in_specs, flops, moved, scratch=(), mib=24):
    outs = jax.tree.map(lambda _: VMEM, out_shape)
    return pl.pallas_call(
        kernel,
        out_shape=out_shape,
        in_specs=in_specs,
        out_specs=outs,
        scratch_shapes=list(scratch),
        compiler_params=pltpu.CompilerParams(vmem_limit_bytes=mib << 20),
        cost_estimate=pl.CostEstimate(flops=flops, bytes_accessed=moved, transcendentals=0),
    )


def shape(dims, kind=BF16):
    return jax.ShapeDtypeStruct(dims, kind)


def stage_kernel(token_ref, grad_ref, id_ref, prob_ref, out_ref):
    out_ref[:TOKENS, :EDGE] = token_ref[:, :EDGE]
    out_ref[TOKENS:, :EDGE] = grad_ref[:, :EDGE]
    lane = iota((TOKENS, 128), 1)
    blank = jnp.zeros((TOKENS, 128 - LAST), F32)
    tail = jnp.concatenate([token_ref[:, EDGE:].astype(F32), blank], axis=1)
    grad_tail = jnp.concatenate([grad_ref[:, EDGE:].astype(F32), blank], axis=1)
    prob = prob_ref[...]
    high = prob.astype(BF16).astype(F32)
    rest = prob - high
    middle = rest.astype(BF16).astype(F32)
    for at, part in enumerate((id_ref[...].astype(F32), high, middle, rest - middle)):
        for k in range(TOPK):
            tail = jnp.where(lane == LAST + TOPK * at + k, part[:, k : k + 1], tail)
    out_ref[:TOKENS, EDGE:] = tail.astype(BF16)
    out_ref[TOKENS:, EDGE:] = grad_tail.astype(BF16)


def pack_kernel(plane_ref, raw_ref, *refs):
    out_refs = refs[-PLANES:]
    routes = raw_ref[:TOKENS, EDGE:].astype(F32)

    def fact(at):
        return routes[:, LAST + at : LAST + at + TOPK]

    ids = fact(0).astype(jnp.int32)
    prob = fact(TOPK) + (fact(2 * TOPK) + fact(3 * TOPK))
    grid = (TOKENS, ROWS)
    row = iota(grid, 1)
    hop = (row * 2731) >> 16
    slot = row - PACKED * hop
    is_grad = slot >= SLOTS
    slot = jnp.where(is_grad, slot - SLOTS, slot)
    expert = GROUP * ((plane_ref[0] + hop) & (PLANES - 1)) + (slot >> 1)
    picked, weight = pick_tokens(ids, prob, expert, slot)
    scale = jnp.sum(picked * weight, axis=0, keepdims=True)
    scale = jnp.where(is_grad[:1], scale, 0.0)
    scale = jnp.broadcast_to(scale, (TOKENS, ROWS)).T[:, :1]
    want_grad = jnp.where(is_grad, 1.0, 0.0).T[:, :1] > 0.5
    picked = picked.T.astype(BF16)
    for at, size in chunks(WIDE):
        end = min(at + size, D)
        value = jnp.where(
            want_grad,
            scale * dot(picked, raw_ref[TOKENS:, at:end], 1, 0),
            dot(picked, raw_ref[:TOKENS, at:end], 1, 0),
        )
        if end < at + size:
            value = jnp.concatenate([value, jnp.zeros((ROWS, at + size - end), F32)], axis=1)
        for k, out_ref in enumerate(out_refs):
            out_ref[:, at : at + size] = value[PACKED * k : PACKED * (k + 1)].astype(BF16)


def pick_tokens(ids, prob, expert, slot):
    has = jnp.zeros(expert.shape, F32)
    weight = jnp.zeros(expert.shape, F32)
    for k in range(TOPK):
        match = ids[:, k : k + 1] == expert
        has = jnp.where(match, 1.0, has)
        weight = jnp.where(match, prob[:, k : k + 1], weight)
    square = (TOKENS, TOKENS)
    earlier = (iota(square, 1) < iota(square, 0)).astype(F32).astype(BF16)
    rank = dot(earlier, has.astype(BF16), 1, 0).astype(jnp.int32)
    wanted = (has > 0.5) & (rank == (slot & 1)) & (slot < SLOTS)
    return jnp.where(wanted, 1.0, 0.0), weight


def local_slot(expert_ref, plane_ref, row):
    local = jnp.zeros(row.shape, jnp.int32)
    for peer in range(PEERS):
        named = expert_ref[plane_ref[0] * PEERS + peer] - GROUP * plane_ref[0]
        local = jnp.where((row >> 4) == peer, named, local)
    return 2 * local + (row & 1)


def pick_kernel(expert_ref, plane_ref, *refs):
    blocks, out_ref = refs[:PLANES], refs[-1]
    grid = (ROWS, ROWS)
    row, column = iota(grid, 0), iota(grid, 1)
    source = PACKED * ((row >> 1) & (PLANES - 1)) + local_slot(expert_ref, plane_ref, row)
    column = column[:, : PLANES * PACKED]
    source = source[:, : PLANES * PACKED]
    pick_row = (column == source).astype(F32).astype(BF16)
    pick_grad = (column == source + SLOTS).astype(F32).astype(BF16)
    for at, size in chunks(WIDE):
        block = jnp.concatenate(
            [ref[:, at : at + size].astype(F32) for ref in blocks], axis=0
        ).astype(BF16)
        for first, picked in ((0, pick_row), (16, pick_grad)):
            value = dot(picked, block, 1, 0).astype(BF16)
            out_ref[:, first : first + 16, at : at + size] = value.reshape(PEERS, 16, size)


def token_part(ref, at=0, end=WIDE):
    return ref[:, :16, at:end].reshape(ROWS, end - at)


def grad_part(ref, at=0, end=D):
    return ref[:, 16:, at:end].reshape(ROWS, end - at)


def shifted(rows):
    return pltpu.roll(rows.astype(F32), LAST, 1).astype(BF16)


def unit_kernel(
    limit_ref, replica_ref, pair_ref, weight_ref, _, own_ref, other_ref, part_ref, shift_ref
):
    rows = token_part(pair_ref)
    shift_ref[...] = shifted(rows)
    gate = dot(weight_ref[:, :WIDE], rows, 1, 1)
    up = dot(weight_ref[:, EDGE : 2 * D], shift_ref[...], 1, 1)
    back = dot(weight_ref[:, 2 * D :], grad_part(pair_ref), 1, 1)
    mask = jnp.where(iota(gate.shape, 0) < limit_ref[0], 1.0, 0.0)
    sigma = jax.nn.sigmoid(gate)
    active = gate * sigma * mask
    hidden = (active * up).astype(BF16)
    grad_gate = (back * up * (sigma * (1.0 + gate * (1.0 - sigma))) * mask).astype(BF16)
    grad_up = (back * active).astype(BF16)
    for half in range(2):
        for target, mine in ((own_ref, half), (other_ref, 1 - half)):

            @pl.when(replica_ref[0] == mine)
            def _(target=target, at=half * HALF):
                target[0] = grad_gate[at : at + HALF]
                target[1] = grad_up[at : at + HALF]
                target[2] = hidden[at : at + HALF]

    gate_rows = grad_gate.astype(F32).T.astype(BF16)
    up_rows = grad_up.astype(F32).T.astype(BF16)
    for at, size in chunks(WIDE):
        end = at + size
        value = dot(gate_rows, weight_ref[:, at:end], 1, 0)
        wide = dot(up_rows, weight_ref[:, EDGE + at : min(EDGE + end + 128, 2 * D)], 1, 0)
        value = value + pltpu.roll(wide, wide.shape[1] - LAST, 1)[:, :size]
        keep = min(end, D) - at
        part_ref[:, at : at + keep] = value[:, :keep].astype(BF16)


def weight_kernel(own_ref, other_ref, pair_ref, far_ref, out_ref, shift_ref, far_shift_ref):
    shift_ref[...] = shifted(token_part(pair_ref))
    far_shift_ref[...] = shifted(token_part(far_ref))

    def term(which, near, far):
        return dot(own_ref[which], near, 1, 0) + dot(other_ref[which], far, 1, 0)

    def gate_term(at, end):
        return term(0, token_part(pair_ref, at, end), token_part(far_ref, at, end))

    def up_term(at, end):
        return term(1, shift_ref[:, at:end], far_shift_ref[:, at:end])

    for at, size in chunks(EDGE):
        value = gate_term(at, at + size)
        out_ref[0, :, at : at + size] = value.astype(BF16)
    value = gate_term(EDGE, WIDE) + up_term(0, 128)
    out_ref[0, :, EDGE:WIDE] = value.astype(BF16)
    for at, size in chunks(WIDE - 128):
        value = up_term(128 + at, 128 + at + size)
        out_ref[0, :, WIDE + at : WIDE + at + size] = value.astype(BF16)
    for at, size in chunks(D):
        value = term(
            2, grad_part(pair_ref, at, at + size), grad_part(far_ref, at, at + size)
        )
        out_ref[0, :, 2 * D + at : 2 * D + at + size] = value.astype(BF16)


def gather_kernel(expert_ref, plane_ref, part_ref, *out_refs):
    grid = (GATHERED, ROWS)
    row, column = iota(grid, 0), iota(grid, 1)
    same_hop = (row >> 4) == ((column >> 1) & (PLANES - 1))
    same_slot = (row & 15) == local_slot(expert_ref, plane_ref, column)
    picked = (same_hop & same_slot).astype(F32).astype(BF16)
    for at, size in chunks(D):
        value = dot(picked, part_ref[:, at : at + size], 1, 0).astype(BF16)
        for k, out_ref in enumerate(out_refs):
            out_ref[:, at : at + size] = value[16 * k : 16 * (k + 1)]


def sum_kernel(plane_ref, id_ref, *refs):
    blocks, out_ref = refs[:PLANES], refs[PLANES]
    row = iota((TOKENS, GATHERED), 1)
    slot = row & 15
    expert = GROUP * ((plane_ref[0] + (row >> 4)) & (PLANES - 1)) + (slot >> 1)
    picked, _ = pick_tokens(id_ref[...], jnp.zeros((TOKENS, TOPK), F32), expert, slot)
    picked = picked.astype(BF16)
    for at, size in chunks(D):
        block = jnp.concatenate([ref[:, at : at + size] for ref in blocks], axis=0)
        out_ref[:, at : at + size] = dot(picked, block, 1, 0).astype(BF16)


def along_z(value, by):
    return lax.ppermute(value, "z", [(i, (i + by) % PLANES) for i in range(PLANES)])


def swap_dp(value):
    return lax.ppermute(value, "dp", [(0, 1), (1, 0)])


def after(value, other):
    return pl.pallas_call(
        lambda *refs: None,
        out_shape=shape(value.shape),
        in_specs=[WAITED, WAITED],
        out_specs=WAITED,
        input_output_aliases={0: 0},
    )(value, other)


def in_plane(blocks):
    return lax.all_to_all(blocks, PLANE, split_axis=0, concat_axis=0, tiled=True)


FAR_FIRST = (4, 3, 5, 2, 6, 1, 7)


def to_planes(blocks):
    sent = {by: along_z(blocks[by], by) for by in FAR_FIRST}
    return [blocks[0]] + [sent[by] for by in range(1, PLANES)]


def shards(tokens, grad_out, route_ids, route_prob, device_expert, unit_count, expert_weights):
    plane = lax.axis_index("z").astype(jnp.int32)
    replica = lax.axis_index("dp").astype(jnp.int32).reshape(1)
    limit = lax.dynamic_slice_in_dim(unit_count, plane * PEERS + lax.axis_index(PLANE), 1)
    slot_weights = expert_weights[0]

    plane = plane.reshape(1)
    row_flops = 2 * ROWS * D
    raw = call(stage_kernel, shape((2 * TOKENS, WIDE)), [VMEM] * 4, 0, 400_000, (), 8)(
        tokens, grad_out, route_ids, route_prob
    )

    def pack(block):
        return call(
            pack_kernel,
            [shape((PACKED, WIDE))] * PLANES,
            [SMEM, VMEM],
            row_flops * TOKENS,
            1_400_000,
            (),
            12,
        )(plane, block)

    def pick(blocks, *earlier):
        return call(
            pick_kernel,
            shape((PEERS, 32, WIDE)),
            [SMEM, SMEM] + [VMEM] * PLANES + [WAITED] * len(earlier),
            2 * row_flops * PLANES * PACKED,
            4_200_000,
            (),
            14,
        )(device_expert, plane, *blocks, *earlier)

    blocks = pack(raw)
    far_blocks = pack(swap_dp(raw))
    pairs = in_plane(pick(to_planes(blocks), far_blocks[0]))
    far_sent = pick(to_planes(far_blocks))

    own, other, part = call(
        unit_kernel,
        (shape((3, HALF, ROWS)), shape((3, HALF, ROWS)), shape((ROWS, D))),
        [SMEM, SMEM, VMEM, VMEM, WAITED],
        5 * row_flops * UNITS,
        14_000_000,
        [pltpu.VMEM((ROWS, WIDE), BF16)],
        40,
    )(limit, replica, pairs, slot_weights, far_sent)
    other = swap_dp(other)

    returned = in_plane(part.reshape(PEERS, 16, D)).reshape(ROWS, D)
    token_parts = call(
        gather_kernel,
        [shape((16, D))] * PLANES,
        [SMEM, SMEM, VMEM],
        row_flops * GATHERED,
        2_400_000,
    )(device_expert, plane, returned)
    home = {by: along_z(token_parts[by], -by) for by in FAR_FIRST}
    home = [token_parts[0]] + [home[by] for by in range(1, PLANES)]
    far_pairs = in_plane(after(far_sent, returned))
    grad_weights = call(
        weight_kernel,
        shape((1, HALF, 3 * D)),
        [VMEM] * 4,
        3 * row_flops * UNITS,
        12_000_000,
        [pltpu.VMEM((ROWS, WIDE), BF16)] * 2,
        40,
    )(own, other, pairs, far_pairs)
    grad_tokens = call(
        sum_kernel, shape((TOKENS, D)), [SMEM] + [VMEM] * (1 + PLANES), row_flops, 900_000
    )(plane, route_ids, *home)
    return grad_tokens, grad_weights


def solution(mesh):
    fine = Mesh(mesh.devices.reshape(2, PLANES, 4, 2, 2), ALL)
    slots = ("z",) + PLANE
    in_specs = (P(ALL), P(ALL), P(ALL), P(ALL), P(), P(), P(slots))
    out_specs = (P(ALL), P(slots, "dp"))
    return jax.shard_map(shards, mesh=fine, in_specs=in_specs, out_specs=out_specs, check_vma=False)
```
